512 devices in a mesh: ctx: 128 (over y, z_lo, x), tp: 4 (over z_hi, core).
Axes of the slice: x: 4, y: 4, z: 16 (z_hi: 2, z_lo: 8; z = z_hi * 8 + z_lo), core: 2. Of those that a mesh axis runs over, the one named last changes fastest.
Arguments:
- query_proj: bfloat16 [16384, 4096], P('ctx', 'tp'), may hold values from -6 to 6
- key_proj: bfloat16 [16384, 4096], P('ctx', 'tp'), may hold values from -6 to 6
- value_proj: bfloat16 [16384, 4096], P('ctx', 'tp'), may hold values from -6 to 6
- cotangent: bfloat16 [16384, 4096], P('ctx', 'tp'), may hold values from -6 to 6
- filter_taps: float32 [16384, 4096], P('ctx', 'tp'), may hold values from -1 to 1
- short_weights: float32 [3, 3, 4096], P(None, None, 'tp'), may hold values from -3.5 to 3.5
Outputs:
- gated_out: bfloat16 [16384, 4096], P('ctx', 'tp')
- query_grad: bfloat16 [16384, 4096], P('ctx', 'tp')
- key_grad: bfloat16 [16384, 4096], P('ctx', 'tp')
- value_grad: bfloat16 [16384, 4096], P('ctx', 'tp')
- filter_grad: float32 [16384, 4096], P('ctx', 'tp')
- short_grad: float32 [3, 3, 4096], P(None, None, 'tp')
The draws below stay inside these ranges and needn't reach their ends.
All inputs are finite; a program needn't handle non-finite values.
Results may differ from the reference program's by a relative error of at most 0.0065.
Values may be sent and summed in bfloat16 or wider, within the bound.
A program may use at most 64 MiB of HBM per device.

```python
import math
import jax
import jax.numpy as jnp
from jax import lax

D = 4096
TAPS = 3
SEQ = 16384


def draw_filter_taps(key, part):
    key_rough, key_pick, key_fast, key_slow = jax.random.split(key, 4)
    positions = jnp.arange(SEQ, dtype=jnp.float32)[:, None]
    rough_part = jax.random.truncated_normal(key_rough, -3.0, 3.0, (SEQ, D), jnp.float32)
    fast_share = 0.5
    fast_pick = jax.random.bernoulli(key_pick, fast_share, (D,))
    fast_len = jax.random.uniform(key_fast, (D,), jnp.float32, 30.0, 50.0)
    slow_len = jnp.exp(jax.random.uniform(key_slow, (D,), jnp.float32, math.log(SEQ / 4.0), math.log(SEQ * 4.0)))
    decay_len = jnp.where(fast_pick, fast_len, slow_len)
    energy = 0.5 * decay_len * (1.0 - jnp.exp(-2.0 * SEQ / decay_len))
    return rough_part * jnp.exp(-positions / decay_len) / jnp.sqrt(energy)


def levels(stream_key, extent, cuts, least, largest):
    loudness, own = 1.0, jax.random.fold_in(stream_key, 6)
    for axis_at, shards_of in cuts:
        heights = jnp.exp(jax.random.uniform(jax.random.fold_in(own, axis_at), (shards_of,), jnp.float32, least / len(cuts), largest / len(cuts)))
        loudness = loudness * jnp.repeat(heights, extent[axis_at] // shards_of).reshape([-1 if axis == axis_at else 1 for axis in range(len(extent))])
    return loudness


def scatter_about(own_key, shape, deviation, most, cuts=(), kind=jnp.bfloat16):
    result = deviation * jax.random.normal(own_key, shape, jnp.float32)
    if cuts:
        result = result * levels(own_key, shape, cuts, -0.22, 0.18)
    return jnp.clip(result, -most, most).astype(kind)


def setup_inputs(seed: int = 0) -> dict:
    arg_keys = jax.random.split(jax.random.key(seed), 7)
    return {
        "query_proj": scatter_about(arg_keys[0], (SEQ, D), 1.0, 6.0, ((0, 128), (1, 4))),
        "key_proj": scatter_about(arg_keys[1], (SEQ, D), 1.0, 6.0, ((0, 128), (1, 4))),
        "value_proj": scatter_about(arg_keys[2], (SEQ, D), 1.0, 6.0, ((0, 128), (1, 4))),
        "cotangent": scatter_about(arg_keys[3], (SEQ, D), 1.0, 6.0, ((0, 128), (1, 4))),
        "filter_taps": draw_filter_taps(jax.random.fold_in(arg_keys[6], 71), 0),
        "short_weights": scatter_about(arg_keys[5], (3, TAPS, D), TAPS ** -0.5, 3.5, ((2, 4),), jnp.float32),
    }


def causal_short(signal, weights):
    length = signal.shape[0]
    padded = jnp.pad(signal, ((TAPS - 1, 0), (0, 0)))
    summed = jnp.zeros_like(signal)
    for offset in range(TAPS):
        summed = summed + weights[offset] * padded[TAPS - 1 - offset:TAPS - 1 - offset + length]
    return summed


def reverse_short(grad_in, weights):
    length = grad_in.shape[0]
    padded = jnp.pad(grad_in, ((0, TAPS - 1), (0, 0)))
    summed = jnp.zeros_like(grad_in)
    for offset in range(TAPS):
        summed = summed + weights[offset] * padded[offset:offset + length]
    return summed


def short_tap_sums(grad_in, signal):
    length = signal.shape[0]
    padded = jnp.pad(signal, ((TAPS - 1, 0), (0, 0)))
    rows = [jnp.sum(grad_in * padded[TAPS - 1 - offset:TAPS - 1 - offset + length], axis=0) for offset in range(TAPS)]
    return jnp.stack(rows, axis=0)


def reference(query_proj, key_proj, value_proj, cotangent, filter_taps, short_weights):
    block_width = min(256, D)
    blocks = D // block_width
    fft_len = 2 * SEQ
    grad_scale = 1.0 / float(SEQ) ** 0.5

    def to_blocks(whole):
        return whole.reshape(SEQ, blocks, block_width).transpose(1, 0, 2)

    weight_blocks = short_weights.reshape(3, TAPS, blocks, block_width).transpose(2, 0, 1, 3)

    def per_block(pieces):
        query_in, key_in, value_in, cot_in, filter_in, weight_in = pieces
        query_short = causal_short(query_in.astype(jnp.float32), weight_in[0])
        key_short = causal_short(key_in.astype(jnp.float32), weight_in[1])
        value_short = causal_short(value_in.astype(jnp.float32), weight_in[2])
        product = (key_short * value_short).astype(jnp.bfloat16)
        prod_spec = jnp.fft.rfft(product.astype(jnp.float32), n=fft_len, axis=0)
        filter_spec = jnp.fft.rfft(filter_in, n=fft_len, axis=0)
        conv_out = jnp.fft.irfft(prod_spec * filter_spec, n=fft_len, axis=0)[:SEQ].astype(jnp.bfloat16)
        conv_wide = conv_out.astype(jnp.float32)
        gated_out = (query_short * conv_wide).astype(jnp.bfloat16)
        cot_wide = cot_in.astype(jnp.float32)
        gate_grad = (cot_wide * query_short).astype(jnp.bfloat16)
        gate_spec = jnp.fft.rfft(gate_grad.astype(jnp.float32), n=fft_len, axis=0)
        conv_grad = jnp.fft.irfft(jnp.conj(filter_spec) * gate_spec, n=fft_len, axis=0)[:SEQ].astype(jnp.bfloat16)
        filter_grad = jnp.fft.irfft(jnp.conj(prod_spec) * gate_spec, n=fft_len, axis=0)[:SEQ] * grad_scale
        grad_wide = conv_grad.astype(jnp.float32)
        query_pre = cot_wide * conv_wide
        key_pre = grad_wide * value_short
        value_pre = grad_wide * key_short
        query_grad = reverse_short(query_pre, weight_in[0]).astype(jnp.bfloat16)
        key_grad = reverse_short(key_pre, weight_in[1]).astype(jnp.bfloat16)
        value_grad = reverse_short(value_pre, weight_in[2]).astype(jnp.bfloat16)
        short_grad = jnp.stack([
            short_tap_sums(query_pre, query_in.astype(jnp.float32)),
            short_tap_sums(key_pre, key_in.astype(jnp.float32)),
            short_tap_sums(value_pre, value_in.astype(jnp.float32))], axis=0) * grad_scale
        return (gated_out, query_grad, key_grad, value_grad, filter_grad.astype(jnp.float32), short_grad)

    results = lax.map(per_block, (to_blocks(query_proj), to_blocks(key_proj), to_blocks(value_proj),
                                  to_blocks(cotangent), to_blocks(filter_taps), weight_blocks))

    def from_blocks(stacked):
        return stacked.transpose(1, 0, 2).reshape(SEQ, D)

    short_grad = results[5].transpose(1, 2, 0, 3).reshape(3, TAPS, D)
    return (from_blocks(results[0]), from_blocks(results[1]), from_blocks(results[2]),
            from_blocks(results[3]), from_blocks(results[4]), short_grad)
```

```python
import functools
import math

import jax
import jax.numpy as jnp
import numpy as np
from jax import lax
from jax.experimental import pallas as pl
from jax.experimental.pallas import tpu as pltpu
from jax.sharding import PartitionSpec as P

MESH = pl.DeviceIdType.MESH
LANES = 128
FACTORS = {128: (4, 8, 4), 16: (2, 4, 2), 8: (2, 2, 2)}
FILTER, PRODUCT, GATE, CONV, DCONV, DFILTER = range(6)
F32, BF16 = jnp.float32, jnp.bfloat16


def halves(table):
    high = table.astype(BF16)
    low = (table - high.astype(np.float64)).astype(BF16)
    return high, low


def tables(factors):
    ys, zs, xs = factors
    blocks = ys * zs * xs
    tokens = LANES
    period = 2 * blocks * tokens
    order = np.arange(blocks).reshape(ys, zs, xs).transpose(0, 2, 1).reshape(-1)
    half = np.arange(blocks) + 0.5
    outer = 2.0 * math.pi / (2 * blocks) * np.outer(half, order)
    fwd_outer = np.concatenate([np.cos(outer), -np.sin(outer)], axis=0)
    inv_outer = np.concatenate([np.cos(outer).T, -np.sin(outer).T], axis=1) * (2.0 / period)
    lane = np.arange(tokens)
    inner = 2.0 * math.pi / tokens * (np.outer(lane, lane) % tokens)
    cos, sin = np.cos(inner), np.sin(inner)
    fwd_inner = np.block([[cos, -sin], [sin, cos]])
    inv_inner = np.block([[cos, sin], [-sin, cos]])
    twist = 2.0 * math.pi / period * np.outer(half, lane)
    twists = np.stack([np.cos(twist), np.sin(twist)]).astype(np.float32)
    fwd_outer = np.concatenate(halves(fwd_outer), axis=1)
    return (
        fwd_outer,
        np.stack(halves(fwd_inner)),
        np.stack(halves(inv_inner)),
        np.stack(halves(inv_outer)),
        twists,
    )


def dot(left, right):
    return jnp.dot(left, right, preferred_element_type=F32)


def split(value):
    high = value.astype(BF16)
    return high, (value - high.astype(F32)).astype(BF16)


def kernel(
    factors, scale,
    q_ref, k_ref, v_ref, cot_ref, taps_ref, weights_ref,
    fwd_outer, fwd_inner, inv_inner, inv_outer, twists,
    gated_ref, qgrad_ref, kgrad_ref, vgrad_ref, fgrad_ref, sgrad_ref,
    halo, ext, shorts, pre, z_out, z_in, p_out, p_in, turn, rows, spec_h, spec_x, spec_g,
    part, part_in, plane, plane_in, total_in,
    halo_send, halo_recv, pre_send, pre_recv, z_send, z_recv, p_send, p_recv,
    part_send, part_recv, plane_send, plane_recv, total_send, total_recv,
):
    ys, zs, xs = factors
    blocks = ys * zs * xs
    groups = ys * xs
    tokens = q_ref.shape[0]
    chans = LANES // groups
    inputs = (q_ref, k_ref, v_ref)
    me = lax.axis_index("ctx")
    my_x = lax.rem(me, xs)
    my_z = lax.rem(me // xs, zs)
    my_y = me // (xs * zs)
    my_g = my_y * xs + my_x
    after = lax.rem(me + 1, blocks)
    before = lax.rem(me + blocks - 1, blocks)

    def at_z(z):
        return (my_y * zs + z) * xs + my_x

    def at_g(g):
        return ((g // xs) * zs + my_z) * xs + lax.rem(g, xs)

    def z_peer(step):
        return lax.rem(my_z + step, zs)

    def g_peer(step):
        return lax.rem(my_g + step, groups)

    def lanes(z):
        return pl.ds(pl.multiple_of(z * LANES, LANES), LANES)

    def send(source, target, send_sem, recv_sem, device):
        return pltpu.make_async_remote_copy(
            src_ref=source, dst_ref=target, send_sem=send_sem, recv_sem=recv_sem,
            device_id={"ctx": device}, device_id_type=MESH,
        )

    def z_copy(unit, z):
        return send(z_out.at[unit, z], z_in.at[unit, my_z], z_send.at[unit, z], z_recv.at[unit, my_z], at_z(z))

    def z_arrival(unit, z):
        return send(z_out.at[unit, z], z_in.at[unit, z], z_send.at[unit, z], z_recv.at[unit, z], at_z(z))

    def p_copy(unit, g):
        return send(p_out.at[unit, g], p_in.at[unit, my_g], p_send.at[unit, g], p_recv.at[unit, my_g], at_g(g))

    def p_arrival(unit, g):
        return send(p_out.at[unit, g], p_in.at[unit, g], p_send.at[unit, g], p_recv.at[unit, g], at_g(g))

    barrier = pltpu.get_barrier_semaphore()

    def greet(device):
        pl.semaphore_signal(barrier, inc=1, device_id={"ctx": device}, device_id_type=MESH)

    @pl.loop(1, zs)
    def _(step):
        greet(at_z(z_peer(step)))

    @pl.loop(1, groups)
    def _(step):
        greet(at_g(g_peer(step)))

    greet(after)
    greet(before)

    @pl.loop(0, zs)
    def _(z):
        z_out[FILTER, z] = taps_ref[:, lanes(z)].astype(BF16)

    z_in[FILTER, my_z] = z_out[FILTER, my_z]
    pl.semaphore_wait(barrier, (zs - 1) + (groups - 1) + 2)

    halo_copies = [
        send(inputs[i].at[pl.ds(tokens - 16, 16)], halo.at[i], halo_send.at[i], halo_recv.at[i], after)
        for i in range(3)
    ]
    for copy in halo_copies:
        copy.start()

    @pl.loop(1, zs)
    def _(step):
        z_copy(FILTER, z_peer(step)).start()

    for copy in halo_copies:
        copy.wait()

    follows = (me > 0).astype(F32)
    precedes = (me < blocks - 1).astype(F32)

    def short_conv(i, z):
        edge = halo[i, :, lanes(z)].astype(F32)[8:] * follows
        ext[i, z, pl.ds(0, 8)] = edge
        ext[i, z, pl.ds(8, tokens)] = inputs[i][:, lanes(z)].astype(F32)
        summed = weights_ref[i, pl.ds(0, 1), lanes(z)] * ext[i, z, pl.ds(8, tokens)]
        for tap in (1, 2):
            summed = summed + weights_ref[i, pl.ds(tap, 1), lanes(z)] * ext[i, z, pl.ds(8 - tap, tokens)]
        shorts[i, z] = summed
        return summed

    def make_product(z):
        return (short_conv(1, z) * short_conv(2, z)).astype(BF16)

    def make_gate(z):
        return (cot_ref[:, lanes(z)].astype(F32) * short_conv(0, z)).astype(BF16)

    def spread(unit, make):
        @pl.loop(1, zs)
        def _(step):
            z = z_peer(step)
            z_out[unit, z] = make(z)
            z_copy(unit, z).start()

        z_in[unit, my_z] = make(my_z)

    spread(PRODUCT, make_product)
    spread(GATE, make_gate)

    def turn_in(unit):
        turn[my_z] = z_in[unit, my_z].astype(F32).T

        @pl.loop(1, zs)
        def _(step):
            z = z_peer(zs - step)
            z_arrival(unit, z).wait_recv()
            turn[z] = z_in[unit, z].astype(F32).T

        def packed(g):
            mine = pl.ds(pl.multiple_of(g * chans, chans), chans)
            return turn[:, mine, :].reshape(zs * chans, tokens).astype(BF16)

        @pl.loop(1, groups)
        def _(step):
            g = g_peer(step)
            p_out[unit, g] = packed(g)
            p_copy(unit, g).start()

        p_in[unit, my_g] = packed(my_g)

    def gather_plane(unit):
        @pl.loop(1, groups)
        def _(step):
            p_arrival(unit, g_peer(groups - step)).wait_recv()

        @pl.loop(0, groups)
        def _(g):
            rows[pl.ds(pl.multiple_of(g * zs * chans, zs * chans), zs * chans), :] = p_in[unit, g].astype(F32)

    def forward(spec):
        for c in range(chans):
            signal = rows[pl.ds(c, blocks, stride=chans), :].astype(BF16)
            outer = dot(fwd_outer[...], jnp.concatenate([signal, signal], axis=0))
            real, imag = outer[:blocks], outer[blocks:]
            cos, sin = twists[0], twists[1]
            high, low = split(jnp.concatenate([real * cos + imag * sin, imag * cos - real * sin], axis=1))
            spec[c] = dot(high, fwd_inner[0]) + dot(low, fwd_inner[0]) + dot(high, fwd_inner[1])

    def inverse(multiply, left, right, factor):
        for c in range(chans):
            high, low = split(multiply(left[c], right[c]))
            inner = dot(high, inv_inner[0]) + dot(low, inv_inner[0]) + dot(high, inv_inner[1])
            real, imag = inner[:, :tokens], inner[:, tokens:]
            cos, sin = twists[0], twists[1]
            high, low = split(jnp.concatenate([real * cos - imag * sin, imag * cos + real * sin], axis=0))
            signal = dot(inv_outer[0], high) + dot(inv_outer[1], high) + dot(inv_outer[0], low)
            if factor != 1.0:
                signal = signal * factor
            rows[pl.ds(c, blocks, stride=chans), :] = signal

    def times(left, right):
        lr, li, rr, ri = left[:, :tokens], left[:, tokens:], right[:, :tokens], right[:, tokens:]
        return jnp.concatenate([lr * rr - li * ri, lr * ri + li * rr], axis=1)

    def conj_times(left, right):
        lr, li, rr, ri = left[:, :tokens], left[:, tokens:], right[:, :tokens], right[:, tokens:]
        return jnp.concatenate([lr * rr + li * ri, lr * ri - li * rr], axis=1)

    def spread_plane(unit):
        def packed(g):
            return rows[pl.ds(pl.multiple_of(g * zs * chans, zs * chans), zs * chans), :].astype(BF16)

        @pl.loop(1, groups)
        def _(step):
            g = g_peer(step)
            p_out[unit, g] = packed(g)
            p_copy(unit, g).start()

        p_in[unit, my_g] = packed(my_g)

    def turn_out(unit):
        gather_plane(unit)

        def turned(z):
            picked = [rows[pl.ds(pl.multiple_of(g * zs * chans + z * chans, chans), chans), :] for g in range(groups)]
            return jnp.concatenate(picked, axis=0).T.astype(BF16)

        @pl.loop(1, zs)
        def _(step):
            z = z_peer(step)
            z_out[unit, z] = turned(z)
            z_copy(unit, z).start()

        z_in[unit, my_z] = turned(my_z)

    turn_in(FILTER)
    gather_plane(FILTER)
    forward(spec_h)
    turn_in(PRODUCT)
    gather_plane(PRODUCT)
    forward(spec_x)
    inverse(times, spec_x, spec_h, 1.0)
    spread_plane(CONV)
    turn_in(GATE)
    turn_out(CONV)
    gather_plane(GATE)
    forward(spec_g)
    inverse(conj_times, spec_h, spec_g, 1.0)
    spread_plane(DCONV)
    inverse(conj_times, spec_x, spec_g, scale)
    spread_plane(DFILTER)
    turn_out(DCONV)
    turn_out(DFILTER)

    def z_wait(unit):
        @pl.loop(1, zs)
        def _(step):
            z_arrival(unit, z_peer(zs - step)).wait_recv()

    def edge_copy(i):
        return send(
            pre.at[i, :, pl.ds(0, 8)], pre.at[i, :, pl.ds(tokens, 8)], pre_send.at[i], pre_recv.at[i], before
        )

    def tap_sums(i, z):
        own = pre[i, z, pl.ds(0, tokens)]
        for tap in range(3):
            summed = jnp.sum(own * ext[i, z, pl.ds(8 - tap, tokens)], axis=0, keepdims=True)
            part[z, pl.ds(3 * i + tap, 1)] = summed * scale

    def reverse_conv(i, out_ref):
        @pl.loop(0, zs)
        def _(z):
            pre[i, z, pl.ds(tokens, 8)] = pre[i, z, pl.ds(tokens, 8)] * precedes
            summed = weights_ref[i, pl.ds(0, 1), lanes(z)] * pre[i, z, pl.ds(0, tokens)]
            for tap in (1, 2):
                summed = summed + weights_ref[i, pl.ds(tap, 1), lanes(z)] * pre[i, z, pl.ds(tap, tokens)]
            out_ref[:, lanes(z)] = summed.astype(BF16)

    z_wait(CONV)

    @pl.loop(0, zs)
    def _(z):
        conv = z_in[CONV, z].astype(F32)
        gated_ref[:, lanes(z)] = (shorts[0, z] * conv).astype(BF16)
        pre[0, z, pl.ds(0, tokens)] = cot_ref[:, lanes(z)].astype(F32) * conv

    edge_copy(0).start()

    @pl.loop(0, zs)
    def _(z):
        part[z] = jnp.zeros_like(part[z])
        tap_sums(0, z)

    edge_copy(0).wait()
    reverse_conv(0, qgrad_ref)

    z_wait(DCONV)

    @pl.loop(0, zs)
    def _(z):
        grad = z_in[DCONV, z].astype(F32)
        pre[1, z, pl.ds(0, tokens)] = grad * shorts[2, z]
        pre[2, z, pl.ds(0, tokens)] = grad * shorts[1, z]

    edge_copy(1).start()
    edge_copy(2).start()

    def part_copy(z, slot):
        return send(part.at[z], part_in.at[slot], part_send.at[z], part_recv.at[slot], at_z(z))

    def plane_copy(g, slot):
        return send(plane, plane_in.at[slot], plane_send.at[g], plane_recv.at[slot], at_g(g))

    def total_copy(z, slot):
        return send(plane, total_in.at[slot], total_send.at[z], total_recv.at[slot], at_z(z))

    @pl.loop(0, zs)
    def _(z):
        tap_sums(1, z)
        tap_sums(2, z)

    @pl.loop(1, zs)
    def _(step):
        part_copy(z_peer(step), my_z).start()

    part_in[my_z] = part[my_z]
    edge_copy(1).wait()
    edge_copy(2).wait()
    reverse_conv(1, kgrad_ref)

    @pl.loop(1, zs)
    def _(step):
        z = z_peer(zs - step)
        part_copy(z, z).wait_recv()

    plane[...] = jnp.sum(part_in[...], axis=0)

    @pl.loop(1, groups)
    def _(step):
        plane_copy(g_peer(step), my_g).start()

    plane_in[my_g] = plane[...]
    reverse_conv(2, vgrad_ref)

    @pl.loop(1, groups)
    def _(step):
        g = g_peer(groups - step)
        plane_copy(g, g).wait()

    plane[...] = jnp.sum(plane_in[...], axis=0)

    @pl.loop(1, zs)
    def _(step):
        total_copy(z_peer(step), my_z).start()

    total_in[my_z] = plane[...]

    z_wait(DFILTER)

    @pl.loop(0, zs)
    def _(z):
        fgrad_ref[:, lanes(z)] = z_in[DFILTER, z].astype(F32)

    @pl.loop(1, zs)
    def _(step):
        z = z_peer(zs - step)
        total_copy(z, z).wait()
        part_copy(z, z).wait_send()

    for z in range(zs):
        for i in range(3):
            sgrad_ref[i, :, z * LANES:(z + 1) * LANES] = total_in[z, 3 * i:3 * i + 3]

    @pl.loop(0, 6)
    def _(unit):
        @pl.loop(1, zs)
        def _(step):
            z_copy(unit, z_peer(step)).wait_send()

        @pl.loop(1, groups)
        def _(step):
            p_copy(unit, g_peer(step)).wait_send()


def shards(factors, query_proj, key_proj, value_proj, cotangent, filter_taps, short_weights):
    ys, zs, xs = factors
    blocks = ys * zs * xs
    groups = ys * xs
    tokens, width = query_proj.shape
    chans = LANES // groups
    scale = 1.0 / math.sqrt(blocks * tokens)
    whole = pl.BlockSpec(memory_space=pltpu.VMEM)
    constants = [jnp.asarray(table) for table in tables(factors)]
    scratch = [
        pltpu.VMEM((3, 16, width), BF16),
        pltpu.VMEM((3, zs, tokens + 8, LANES), F32),
        pltpu.VMEM((3, zs, tokens, LANES), F32),
        pltpu.VMEM((3, zs, tokens + 8, LANES), F32),
        pltpu.VMEM((6, zs, tokens, LANES), BF16),
        pltpu.VMEM((6, zs, tokens, LANES), BF16),
        pltpu.VMEM((6, groups, zs * chans, tokens), BF16),
        pltpu.VMEM((6, groups, zs * chans, tokens), BF16),
        pltpu.VMEM((zs, LANES, tokens), F32),
        pltpu.VMEM((blocks * chans, tokens), F32),
        pltpu.VMEM((chans, blocks, 2 * tokens), F32),
        pltpu.VMEM((chans, blocks, 2 * tokens), F32),
        pltpu.VMEM((chans, blocks, 2 * tokens), F32),
        pltpu.VMEM((zs, 16, LANES), F32),
        pltpu.VMEM((zs, 16, LANES), F32),
        pltpu.VMEM((16, LANES), F32),
        pltpu.VMEM((groups, 16, LANES), F32),
        pltpu.VMEM((zs, 16, LANES), F32),
    ]
    for shape in (
        (3,), (3,), (3,), (3,), (6, zs), (6, zs), (6, groups), (6, groups),
        (zs,), (zs,), (groups,), (groups,), (zs,), (zs,),
    ):
        scratch.append(pltpu.SemaphoreType.DMA(shape))
    token_out = jax.ShapeDtypeStruct((tokens, width), BF16)
    return pl.pallas_call(
        functools.partial(kernel, factors, scale),
        out_shape=(
            token_out, token_out, token_out, token_out,
            jax.ShapeDtypeStruct((tokens, width), F32),
            jax.ShapeDtypeStruct(short_weights.shape, F32),
        ),
        in_specs=[whole] * 11,
        out_specs=(whole,) * 6,
        scratch_shapes=scratch,
        compiler_params=pltpu.CompilerParams(
            collective_id=0, has_side_effects=True, vmem_limit_bytes=48 * 1024 * 1024
        ),
    )(query_proj, key_proj, value_proj, cotangent, filter_taps, short_weights, *constants)


def solution(mesh):
    rows = P("ctx", "tp")
    weights = P(None, None, "tp")
    return jax.shard_map(
        functools.partial(shards, FACTORS[mesh.shape["ctx"]]),
        mesh=mesh,
        in_specs=(rows, rows, rows, rows, rows, weights),
        out_specs=(rows, rows, rows, rows, rows, weights),
        check_vma=False,
    )
```

```python
import functools
import math

import jax
import jax.numpy as jnp
import numpy as np
from jax import lax
from jax.experimental import pallas as pl
from jax.experimental.pallas import tpu as pltpu
from jax.sharding import PartitionSpec as P

MESH = pl.DeviceIdType.MESH
LANES = 128
VMEM_BYTES = 60 * 1024 * 1024
FACTORS = {128: (4, 8, 4), 16: (2, 4, 2), 8: (2, 2, 2)}
FILTER, PRODUCT, GATE, CONV, DCONV, DFILTER = range(6)
F32, BF16 = jnp.float32, jnp.bfloat16


def halves(table):
    high = table.astype(BF16)
    low = (table - high.astype(np.float64)).astype(BF16)
    return high, low


def tables(factors):
    ys, zs, xs = factors
    blocks = ys * zs * xs
    tokens = LANES
    period = 2 * blocks * tokens
    order = np.arange(blocks).reshape(ys, zs, xs).transpose(0, 2, 1).reshape(-1)
    half = np.arange(blocks) + 0.5
    outer = 2.0 * math.pi / (2 * blocks) * np.outer(half, order)
    fwd_outer = np.concatenate([np.cos(outer), -np.sin(outer)], axis=0)
    inv_outer = np.concatenate([np.cos(outer).T, -np.sin(outer).T], axis=1) * (2.0 / period)
    lane = np.arange(tokens)
    inner = 2.0 * math.pi / tokens * (np.outer(lane, lane) % tokens)
    cos, sin = np.cos(inner), np.sin(inner)
    fwd_inner = np.block([[cos, -sin], [sin, cos]])
    inv_inner = np.block([[cos, sin], [-sin, cos]])
    twist = 2.0 * math.pi / period * np.outer(half, lane)
    twists = np.stack([np.cos(twist), np.sin(twist)]).astype(np.float32)
    fwd_outer = np.concatenate(halves(fwd_outer), axis=1)
    return (
        fwd_outer,
        np.stack(halves(fwd_inner)),
        np.stack(halves(inv_inner)),
        np.stack(halves(inv_outer)),
        twists,
    )


def dot(left, right):
    return jnp.dot(left, right, preferred_element_type=F32)


def split(value):
    high = value.astype(BF16)
    return high, (value - high.astype(F32)).astype(BF16)


def kernel(
    factors, scale,
    q_hbm, k_hbm, v_hbm, cot_hbm, taps_hbm, weights_hbm,
    fwd_outer_hbm, fwd_inner_hbm, inv_inner_hbm, inv_outer_hbm, twists_hbm,
    gated_hbm, qgrad_hbm, kgrad_hbm, vgrad_hbm, fgrad_hbm, sgrad_hbm,
    q_ref, k_ref, v_ref, cot_ref, taps_ref, weights_ref,
    fwd_outer, fwd_inner, inv_inner, inv_outer, twists,
    gated_ref, qgrad_ref, kgrad_ref, vgrad_ref, fgrad_ref, sgrad_ref,
    halo, ext, shorts, pre, z_out, z_in, p_out, p_in, turn, rows, spec_h, spec_x, spec_g,
    part, part_in, plane, line_in, total, total_in,
    load, unload, halo_send, halo_recv, pre_send, pre_recv, z_send, z_recv, p_send, p_recv,
    part_send, part_recv, line_send, line_recv, total_send, total_recv,
):
    ys, zs, xs = factors
    blocks = ys * zs * xs
    groups = ys * xs
    tokens = q_ref.shape[0]
    chans = LANES // groups
    inputs = (q_ref, k_ref, v_ref)
    me = lax.axis_index("ctx")
    my_x = lax.rem(me, xs)
    my_z = lax.rem(me // xs, zs)
    my_y = me // (xs * zs)
    my_g = my_y * xs + my_x
    after = lax.rem(me + 1, blocks)
    before = lax.rem(me + blocks - 1, blocks)

    def at_z(z):
        return (my_y * zs + z) * xs + my_x

    def at_g(g):
        return ((g // xs) * zs + my_z) * xs + lax.rem(g, xs)

    def z_peer(step):
        return lax.rem(my_z + step, zs)

    def g_peer(step):
        return lax.rem(my_g + step, groups)

    def lanes(z):
        return pl.ds(pl.multiple_of(z * LANES, LANES), LANES)

    def send(source, target, send_sem, recv_sem, device):
        return pltpu.make_async_remote_copy(
            src_ref=source, dst_ref=target, send_sem=send_sem, recv_sem=recv_sem,
            device_id={"ctx": device}, device_id_type=MESH,
        )

    def z_copy(unit, z):
        return send(z_out.at[unit, z], z_in.at[unit, my_z], z_send.at[unit, z], z_recv.at[unit, my_z], at_z(z))

    def z_arrival(unit, z):
        return send(z_out.at[unit, z], z_in.at[unit, z], z_send.at[unit, z], z_recv.at[unit, z], at_z(z))

    def p_copy(unit, g):
        return send(p_out.at[unit, g], p_in.at[unit, my_g], p_send.at[unit, g], p_recv.at[unit, my_g], at_g(g))

    def p_arrival(unit, g):
        return send(p_out.at[unit, g], p_in.at[unit, g], p_send.at[unit, g], p_recv.at[unit, g], at_g(g))

    loads = [
        pltpu.make_async_copy(source, target, load.at[i])
        for i, (source, target) in enumerate((
            (taps_hbm, taps_ref), (q_hbm, q_ref), (k_hbm, k_ref), (v_hbm, v_ref), (weights_hbm, weights_ref),
            (cot_hbm, cot_ref), (fwd_outer_hbm, fwd_outer), (fwd_inner_hbm, fwd_inner), (twists_hbm, twists),
            (inv_inner_hbm, inv_inner), (inv_outer_hbm, inv_outer),
        ))
    ]
    for copy in loads:
        copy.start()

    unloads = [
        pltpu.make_async_copy(source, target, unload.at[i])
        for i, (source, target) in enumerate((
            (gated_ref, gated_hbm), (qgrad_ref, qgrad_hbm), (kgrad_ref, kgrad_hbm), (vgrad_ref, vgrad_hbm),
            (fgrad_ref, fgrad_hbm), (sgrad_ref, sgrad_hbm),
        ))
    ]

    barrier = pltpu.get_barrier_semaphore()

    def greet(device):
        pl.semaphore_signal(barrier, inc=1, device_id={"ctx": device}, device_id_type=MESH)

    @pl.loop(1, zs)
    def _(step):
        greet(at_z(z_peer(step)))

    @pl.loop(1, groups)
    def _(step):
        greet(at_g(g_peer(step)))

    greet(after)
    greet(before)
    loads[0].wait()

    @pl.loop(0, zs)
    def _(z):
        z_out[FILTER, z] = taps_ref[:, lanes(z)].astype(BF16)

    z_in[FILTER, my_z] = z_out[FILTER, my_z]
    for copy in loads[1:6]:
        copy.wait()
    pl.semaphore_wait(barrier, (zs - 1) + (groups - 1) + 2)

    halo_copies = [
        send(inputs[i].at[pl.ds(tokens - 16, 16)], halo.at[i], halo_send.at[i], halo_recv.at[i], after)
        for i in range(3)
    ]
    for copy in halo_copies:
        copy.start()

    @pl.loop(1, zs)
    def _(step):
        z_copy(FILTER, z_peer(step)).start()

    for copy in halo_copies:
        copy.wait()

    follows = (me > 0).astype(F32)
    precedes = (me < blocks - 1).astype(F32)

    def short_conv(i, z):
        edge = halo[i, :, lanes(z)].astype(F32)[8:] * follows
        ext[i, z, pl.ds(0, 8)] = edge
        ext[i, z, pl.ds(8, tokens)] = inputs[i][:, lanes(z)].astype(F32)
        summed = weights_ref[i, pl.ds(0, 1), lanes(z)] * ext[i, z, pl.ds(8, tokens)]
        for tap in (1, 2):
            summed = summed + weights_ref[i, pl.ds(tap, 1), lanes(z)] * ext[i, z, pl.ds(8 - tap, tokens)]
        shorts[i, z] = summed
        return summed

    def make_product(z):
        return (short_conv(1, z) * short_conv(2, z)).astype(BF16)

    def make_gate(z):
        return (cot_ref[:, lanes(z)].astype(F32) * short_conv(0, z)).astype(BF16)

    def packed(g):
        mine = pl.ds(pl.multiple_of(g * chans, chans), chans)
        return turn[:, mine, :].reshape(zs * chans, tokens).astype(BF16)

    def picked(z):
        parts = [rows[pl.ds(pl.multiple_of((g * zs + z) * chans, chans), chans), :] for g in range(groups)]
        return jnp.concatenate(parts, axis=0)

    def to_plane(unit):
        @pl.loop(1, groups)
        def _(step):
            g = g_peer(step)
            p_out[unit, g] = packed(g)
            p_copy(unit, g).start()

        p_in[unit, my_g] = packed(my_g)

    def from_plane(unit):
        @pl.loop(1, groups)
        def _(step):
            p_arrival(unit, g_peer(groups - step)).wait_recv()

        @pl.loop(0, groups)
        def _(g):
            rows[pl.ds(pl.multiple_of(g * zs * chans, zs * chans), zs * chans), :] = p_in[unit, g].astype(F32)

    def to_line(unit, block, held_back=0):
        @pl.loop(1, zs - held_back)
        def _(step):
            z = z_peer(step)
            z_out[unit, z] = block(z).astype(BF16)
            z_copy(unit, z).start()

        if held_back:
            @pl.loop(zs - held_back, zs)
            def _(step):
                z = z_peer(step)
                z_out[unit, z] = block(z).astype(BF16)

        z_in[unit, my_z] = block(my_z).astype(BF16)

    def send_held_back(unit, held_back):
        @pl.loop(zs - held_back, zs)
        def _(step):
            z_copy(unit, z_peer(step)).start()

    def from_line(unit, use):
        use(my_z, z_in[unit, my_z].astype(F32))

        @pl.loop(1, zs)
        def _(step):
            z = z_peer(zs - step)
            z_arrival(unit, z).wait_recv()
            use(z, z_in[unit, z].astype(F32))

    def keep(z, block):
        turn[z] = block

    def keep_turned(z, block):
        turn[z] = block.T

    def keep_rows(z, block):
        for g in range(groups):
            rows[pl.ds(pl.multiple_of((g * zs + z) * chans, chans), chans), :] = block[g * chans:(g + 1) * chans]

    def picked_turned(z):
        return picked(z).T

    def forward(spec):
        for c in range(chans):
            signal = rows[pl.ds(c, blocks, stride=chans), :].astype(BF16)
            outer = dot(fwd_outer[...], jnp.concatenate([signal, signal], axis=0))
            real, imag = outer[:blocks], outer[blocks:]
            cos, sin = twists[0], twists[1]
            high, low = split(jnp.concatenate([real * cos + imag * sin, imag * cos - real * sin], axis=1))
            spec[c] = dot(high, fwd_inner[0]) + dot(low, fwd_inner[0]) + dot(high, fwd_inner[1])

    def inverse(multiply, left, right, factor):
        for c in range(chans):
            high, low = split(multiply(left[c], right[c]))
            inner = dot(high, inv_inner[0]) + dot(low, inv_inner[0]) + dot(high, inv_inner[1])
            real, imag = inner[:, :tokens], inner[:, tokens:]
            cos, sin = twists[0], twists[1]
            high, low = split(jnp.concatenate([real * cos - imag * sin, imag * cos + real * sin], axis=0))
            signal = dot(inv_outer[0], high) + dot(inv_outer[1], high) + dot(inv_outer[0], low)
            if factor != 1.0:
                signal = signal * factor
            rows[pl.ds(c, blocks, stride=chans), :] = signal

    def times(left, right):
        lr, li, rr, ri = left[:, :tokens], left[:, tokens:], right[:, :tokens], right[:, tokens:]
        return jnp.concatenate([lr * rr - li * ri, lr * ri + li * rr], axis=1)

    def conj_times(left, right):
        lr, li, rr, ri = left[:, :tokens], left[:, tokens:], right[:, :tokens], right[:, tokens:]
        return jnp.concatenate([lr * rr + li * ri, lr * ri - li * rr], axis=1)

    def rows_to_plane(unit):
        def block(g):
            return rows[pl.ds(pl.multiple_of(g * zs * chans, zs * chans), zs * chans), :].astype(BF16)

        @pl.loop(1, groups)
        def _(step):
            g = g_peer(step)
            p_out[unit, g] = block(g)
            p_copy(unit, g).start()

        p_in[unit, my_g] = block(my_g)

    for unit, make in ((PRODUCT, make_product), (GATE, make_gate)):
        @pl.loop(0, zs)
        def _(z):
            keep_turned(z, make(z).astype(F32))

        to_plane(unit)

    for copy in loads[6:]:
        copy.wait()
    from_plane(PRODUCT)
    to_line(PRODUCT, picked)
    from_line(FILTER, keep_turned)
    to_plane(FILTER)
    from_plane(GATE)
    to_line(GATE, picked)
    from_plane(FILTER)
    forward(spec_h)
    from_line(PRODUCT, keep_rows)
    forward(spec_x)
    inverse(times, spec_x, spec_h, 1.0)
    to_line(CONV, picked)
    from_line(GATE, keep_rows)
    forward(spec_g)
    inverse(conj_times, spec_h, spec_g, 1.0)
    rows_to_plane(DCONV)
    inverse(conj_times, spec_x, spec_g, scale)
    rows_to_plane(DFILTER)
    from_plane(DCONV)
    to_line(DCONV, picked_turned)
    from_plane(DFILTER)
    late = 3 * zs // 8
    to_line(DFILTER, picked_turned, late)
    from_line(CONV, keep)
    to_plane(CONV)

    def z_wait(unit):
        @pl.loop(1, zs)
        def _(step):
            z_arrival(unit, z_peer(zs - step)).wait_recv()

    def edge_copy(i):
        return send(
            pre.at[i, :, pl.ds(0, 8)], pre.at[i, :, pl.ds(tokens, 8)], pre_send.at[i], pre_recv.at[i], before
        )

    def tap_sums(i, z):
        own = pre[i, z, pl.ds(0, tokens)]
        for tap in range(3):
            summed = jnp.sum(own * ext[i, z, pl.ds(8 - tap, tokens)], axis=0, keepdims=True)
            part[3 * i + tap, pl.ds(z, 1)] = summed * scale

    def reverse_conv(i, out_ref):
        @pl.loop(0, zs)
        def _(z):
            pre[i, z, pl.ds(tokens, 8)] = pre[i, z, pl.ds(tokens, 8)] * precedes
            summed = weights_ref[i, pl.ds(0, 1), lanes(z)] * pre[i, z, pl.ds(0, tokens)]
            for tap in (1, 2):
                summed = summed + weights_ref[i, pl.ds(tap, 1), lanes(z)] * pre[i, z, pl.ds(tap, tokens)]
            out_ref[:, lanes(z)] = summed.astype(BF16)

    from_plane(CONV)

    @pl.loop(0, zs)
    def _(z):
        conv = picked_turned(z)
        gated_ref[:, lanes(z)] = (shorts[0, z] * conv).astype(BF16)
        pre[0, z, pl.ds(0, tokens)] = cot_ref[:, lanes(z)].astype(F32) * conv

    unloads[0].start()
    edge_copy(0).start()
    part[...] = jnp.zeros_like(part)

    @pl.loop(0, zs)
    def _(z):
        tap_sums(0, z)

    edge_copy(0).wait()
    reverse_conv(0, qgrad_ref)
    unloads[1].start()

    z_wait(DCONV)

    @pl.loop(0, zs)
    def _(z):
        grad = z_in[DCONV, z].astype(F32)
        pre[1, z, pl.ds(0, tokens)] = grad * shorts[2, z]
        pre[2, z, pl.ds(0, tokens)] = grad * shorts[1, z]

    edge_copy(1).start()
    edge_copy(2).start()

    share = part.shape[0] // groups

    def shares(g):
        return pl.ds(g * share, share)

    def part_copy(g, slot):
        return send(part.at[shares(g)], part_in.at[slot], part_send.at[g], part_recv.at[slot], at_g(g))

    def line_copy(z, slot):
        return send(plane, line_in.at[slot], line_send.at[z], line_recv.at[slot], at_z(z))

    def total_copy(g, slot):
        return send(total, total_in.at[shares(slot)], total_send.at[g], total_recv.at[slot], at_g(g))

    @pl.loop(0, zs)
    def _(z):
        tap_sums(1, z)
        tap_sums(2, z)

    @pl.loop(1, groups)
    def _(step):
        part_copy(g_peer(step), my_g).start()

    part_in[my_g] = part[shares(my_g)]

    @pl.loop(1, groups)
    def _(step):
        g = g_peer(groups - step)
        part_copy(g, g).wait_recv()

    plane[...] = jnp.sum(part_in[...], axis=0)

    @pl.loop(1, zs)
    def _(step):
        line_copy(z_peer(step), my_z).start()

    line_in[my_z] = plane[...]
    send_held_back(DFILTER, late)
    edge_copy(1).wait()
    reverse_conv(1, kgrad_ref)
    unloads[2].start()
    edge_copy(2).wait()
    reverse_conv(2, vgrad_ref)
    unloads[3].start()

    @pl.loop(1, zs)
    def _(step):
        z = z_peer(zs - step)
        line_copy(z, z).wait_recv()

    total[...] = jnp.sum(line_in[...], axis=0)

    @pl.loop(1, groups)
    def _(step):
        total_copy(g_peer(step), my_g).start()

    total_in[shares(my_g)] = total[...]

    z_wait(DFILTER)

    @pl.loop(0, zs)
    def _(z):
        fgrad_ref[:, lanes(z)] = z_in[DFILTER, z].astype(F32)

    unloads[4].start()

    @pl.loop(1, groups)
    def _(step):
        g = g_peer(groups - step)
        total_copy(g, g).wait()
        part_copy(g, g).wait_send()

    for z in range(zs):
        for i in range(3):
            for tap in range(3):
                sgrad_ref[i, tap:tap + 1, z * LANES:(z + 1) * LANES] = total_in[3 * i + tap, z:z + 1]

    unloads[5].start()

    @pl.loop(1, zs)
    def _(step):
        line_copy(z_peer(step), my_z).wait_send()

    @pl.loop(0, 6)
    def _(unit):
        @pl.loop(1, zs)
        def _(step):
            z_copy(unit, z_peer(step)).wait_send()

        @pl.loop(1, groups)
        def _(step):
            p_copy(unit, g_peer(step)).wait_send()

    for copy in unloads:
        copy.wait()


def store(*refs):
    *refs, sems = refs
    count = len(refs) // 3
    sources, targets, held = refs[:count], refs[count:2 * count], refs[2 * count:]
    loads = [pltpu.make_async_copy(sources[i], held[i], sems.at[0, i]) for i in range(count)]
    stores = [pltpu.make_async_copy(held[i], targets[i], sems.at[1, i]) for i in range(count)]
    for copy in loads:
        copy.start()
    for load, copy in zip(loads, stores):
        load.wait()
        copy.start()
    for copy in stores:
        copy.wait()


def shards(factors, query_proj, key_proj, value_proj, cotangent, filter_taps, short_weights):
    ys, zs, xs = factors
    blocks = ys * zs * xs
    groups = ys * xs
    tokens, width = query_proj.shape
    chans = LANES // groups
    scale = 1.0 / math.sqrt(blocks * tokens)
    far = pl.BlockSpec(memory_space=pltpu.HBM)
    constants = [jnp.asarray(table) for table in tables(factors)]
    operands = (query_proj, key_proj, value_proj, cotangent, filter_taps, short_weights, *constants)
    token_out = jax.ShapeDtypeStruct((tokens, width), BF16)
    outs = (
        token_out, token_out, token_out, token_out,
        jax.ShapeDtypeStruct((tokens, width), F32),
        jax.ShapeDtypeStruct(short_weights.shape, F32),
    )
    share = -(-9 // groups)
    scratch = [pltpu.VMEM(array.shape, array.dtype) for array in (*operands, *outs)]
    scratch += [
        pltpu.VMEM((3, 16, width), BF16),
        pltpu.VMEM((3, zs, tokens + 8, LANES), F32),
        pltpu.VMEM((3, zs, tokens, LANES), F32),
        pltpu.VMEM((3, zs, tokens + 8, LANES), F32),
        pltpu.VMEM((6, zs, tokens, LANES), BF16),
        pltpu.VMEM((6, zs, tokens, LANES), BF16),
        pltpu.VMEM((6, groups, zs * chans, tokens), BF16),
        pltpu.VMEM((6, groups, zs * chans, tokens), BF16),
        pltpu.VMEM((zs, LANES, tokens), F32),
        pltpu.VMEM((blocks * chans, tokens), F32),
        pltpu.VMEM((chans, blocks, 2 * tokens), F32),
        pltpu.VMEM((chans, blocks, 2 * tokens), F32),
        pltpu.VMEM((chans, blocks, 2 * tokens), F32),
        pltpu.VMEM((groups * share, zs, LANES), F32),
        pltpu.VMEM((groups, share, zs, LANES), F32),
        pltpu.VMEM((share, zs, LANES), F32),
        pltpu.VMEM((zs, share, zs, LANES), F32),
        pltpu.VMEM((share, zs, LANES), F32),
        pltpu.VMEM((groups * share, zs, LANES), F32),
    ]
    for shape in (
        (len(operands),), (len(outs),), (3,), (3,), (3,), (3,), (6, zs), (6, zs), (6, groups), (6, groups),
        (groups,), (groups,), (zs,), (zs,), (groups,), (groups,),
    ):
        scratch.append(pltpu.SemaphoreType.DMA(shape))
    results = pl.pallas_call(
        functools.partial(kernel, factors, scale),
        out_shape=outs,
        in_specs=[far] * len(operands),
        out_specs=(far,) * len(outs),
        scratch_shapes=scratch,
        compiler_params=pltpu.CompilerParams(
            collective_id=0, has_side_effects=True, vmem_limit_bytes=VMEM_BYTES
        ),
    )(*operands)
    return pl.pallas_call(
        store,
        out_shape=outs,
        in_specs=[far] * len(outs),
        out_specs=(far,) * len(outs),
        scratch_shapes=[pltpu.VMEM(out.shape, out.dtype) for out in outs] + [pltpu.SemaphoreType.DMA((2, len(outs)))],
    )(*results)


def solution(mesh):
    rows = P("ctx", "tp")
    weights = P(None, None, "tp")
    return jax.shard_map(
        functools.partial(shards, FACTORS[mesh.shape["ctx"]]),
        mesh=mesh,
        in_specs=(rows, rows, rows, rows, rows, weights),
        out_specs=(rows, rows, rows, rows, rows, weights),
        check_vma=False,
    )
```

```python
import functools
import math

import jax
import jax.numpy as jnp
import numpy as np
from jax import lax
from jax.experimental import pallas as pl
from jax.experimental.pallas import tpu as pltpu
from jax.sharding import PartitionSpec as P

MESH = pl.DeviceIdType.MESH
LANES = 128
VMEM_BYTES = 60 * 1024 * 1024
FACTORS = {128: (4, 8, 4), 16: (2, 4, 2), 8: (2, 2, 2)}
FILTER, PRODUCT, GATE, CONV, DCONV, DFILTER = range(6)
F32, BF16 = jnp.float32, jnp.bfloat16


def halves(table):
    high = table.astype(BF16)
    low = (table - high.astype(np.float64)).astype(BF16)
    return high, low


def tables(factors):
    ys, zs, xs = factors
    blocks = ys * zs * xs
    tokens = LANES
    period = 2 * blocks * tokens
    order = np.arange(blocks).reshape(ys, zs, xs).transpose(0, 2, 1).reshape(-1)
    half = np.arange(blocks) + 0.5
    outer = 2.0 * math.pi / (2 * blocks) * np.outer(half, order)
    fwd_outer = np.concatenate([np.cos(outer), -np.sin(outer)], axis=0)
    inv_outer = np.concatenate([np.cos(outer).T, -np.sin(outer).T], axis=1) * (2.0 / period)
    lane = np.arange(tokens)
    inner = 2.0 * math.pi / tokens * (np.outer(lane, lane) % tokens)
    cos, sin = np.cos(inner), np.sin(inner)
    fwd_inner = np.block([[cos, -sin], [sin, cos]])
    inv_inner = np.block([[cos, sin], [-sin, cos]])
    twist = 2.0 * math.pi / period * np.outer(half, lane)
    twists = np.stack([np.cos(twist), np.sin(twist)]).astype(np.float32)
    fwd_outer = np.concatenate(halves(fwd_outer), axis=1)
    return (
        fwd_outer,
        np.stack(halves(fwd_inner)),
        np.stack(halves(inv_inner)),
        np.stack(halves(inv_outer)),
        twists,
    )


def dot(left, right):
    return jnp.dot(left, right, preferred_element_type=F32)


def split(value):
    high = value.astype(BF16)
    return high, (value - high.astype(F32)).astype(BF16)


def kernel(
    factors, scale,
    q_hbm, k_hbm, v_hbm, cot_hbm, taps_hbm, weights_hbm,
    fwd_outer_hbm, fwd_inner_hbm, inv_inner_hbm, inv_outer_hbm, twists_hbm,
    gated_hbm, qgrad_hbm, kgrad_hbm, vgrad_hbm, fgrad_hbm, sgrad_hbm,
    q_ref, k_ref, v_ref, cot_ref, taps_ref, weights_ref,
    fwd_outer, fwd_inner, inv_inner, inv_outer, twists,
    gated_ref, qgrad_ref, kgrad_ref, vgrad_ref, fgrad_ref, sgrad_ref,
    halo, ext, shorts, pre, z_out, z_in, p_out, p_in, turn, rows, spec_h, spec_x, spec_g,
    part, part_in, plane, line_in, total, total_in,
    load, unload, halo_send, halo_recv, pre_send, pre_recv, z_send, z_recv, p_send, p_recv,
    part_send, part_recv, line_send, line_recv, total_send, total_recv,
):
    ys, zs, xs = factors
    blocks = ys * zs * xs
    groups = ys * xs
    tokens = q_ref.shape[0]
    chans = LANES // groups
    inputs = (q_ref, k_ref, v_ref)
    me = lax.axis_index("ctx")
    my_x = lax.rem(me, xs)
    my_z = lax.rem(me // xs, zs)
    my_y = me // (xs * zs)
    my_g = my_y * xs + my_x
    after = lax.rem(me + 1, blocks)
    before = lax.rem(me + blocks - 1, blocks)

    def at_z(z):
        return (my_y * zs + z) * xs + my_x

    def at_g(g):
        return ((g // xs) * zs + my_z) * xs + lax.rem(g, xs)

    def z_peer(step):
        return lax.rem(my_z + step, zs)

    def g_peer(step):
        return lax.rem(my_g + step, groups)

    def lanes(z):
        return pl.ds(pl.multiple_of(z * LANES, LANES), LANES)

    def send(source, target, send_sem, recv_sem, device):
        return pltpu.make_async_remote_copy(
            src_ref=source, dst_ref=target, send_sem=send_sem, recv_sem=recv_sem,
            device_id={"ctx": device}, device_id_type=MESH,
        )

    def z_copy(unit, z):
        return send(z_out.at[unit, z], z_in.at[unit, my_z], z_send.at[unit, z], z_recv.at[unit, my_z], at_z(z))

    def z_arrival(unit, z):
        return send(z_out.at[unit, z], z_in.at[unit, z], z_send.at[unit, z], z_recv.at[unit, z], at_z(z))

    def p_copy(unit, g):
        return send(p_out.at[unit, g], p_in.at[unit, my_g], p_send.at[unit, g], p_recv.at[unit, my_g], at_g(g))

    def p_arrival(unit, g):
        return send(p_out.at[unit, g], p_in.at[unit, g], p_send.at[unit, g], p_recv.at[unit, g], at_g(g))

    loads = [
        pltpu.make_async_copy(source, target, load.at[i])
        for i, (source, target) in enumerate((
            (taps_hbm, taps_ref), (q_hbm, q_ref), (k_hbm, k_ref), (v_hbm, v_ref), (weights_hbm, weights_ref),
            (cot_hbm, cot_ref), (fwd_outer_hbm, fwd_outer), (fwd_inner_hbm, fwd_inner), (twists_hbm, twists),
            (inv_inner_hbm, inv_inner), (inv_outer_hbm, inv_outer),
        ))
    ]
    for copy in loads:
        copy.start()

    unloads = [
        pltpu.make_async_copy(source, target, unload.at[i])
        for i, (source, target) in enumerate((
            (gated_ref, gated_hbm), (qgrad_ref, qgrad_hbm), (kgrad_ref, kgrad_hbm), (vgrad_ref, vgrad_hbm),
            (fgrad_ref, fgrad_hbm), (sgrad_ref, sgrad_hbm),
        ))
    ]

    barrier = pltpu.get_barrier_semaphore()

    def greet(device):
        pl.semaphore_signal(barrier, inc=1, device_id={"ctx": device}, device_id_type=MESH)

    @pl.loop(1, zs)
    def _(step):
        greet(at_z(z_peer(step)))

    @pl.loop(1, groups)
    def _(step):
        greet(at_g(g_peer(step)))

    greet(after)
    greet(before)
    loads[0].wait()

    @pl.loop(0, zs)
    def _(z):
        z_out[FILTER, z] = taps_ref[:, lanes(z)].astype(BF16)

    z_in[FILTER, my_z] = z_out[FILTER, my_z]
    for copy in loads[1:6]:
        copy.wait()
    pl.semaphore_wait(barrier, (zs - 1) + (groups - 1) + 2)

    halo_copies = [
        send(inputs[i].at[pl.ds(tokens - 16, 16)], halo.at[i], halo_send.at[i], halo_recv.at[i], after)
        for i in range(3)
    ]
    for copy in halo_copies:
        copy.start()

    @pl.loop(1, zs)
    def _(step):
        z_copy(FILTER, z_peer(step)).start()

    for copy in halo_copies:
        copy.wait()

    follows = (me > 0).astype(F32)
    precedes = (me < blocks - 1).astype(F32)

    def short_conv(i, z):
        edge = halo[i, :, lanes(z)].astype(F32)[8:] * follows
        ext[i, z, pl.ds(0, 8)] = edge
        ext[i, z, pl.ds(8, tokens)] = inputs[i][:, lanes(z)].astype(F32)
        summed = weights_ref[i, pl.ds(0, 1), lanes(z)] * ext[i, z, pl.ds(8, tokens)]
        for tap in (1, 2):
            summed = summed + weights_ref[i, pl.ds(tap, 1), lanes(z)] * ext[i, z, pl.ds(8 - tap, tokens)]
        shorts[i, z] = summed
        return summed

    def make_product(z):
        return (short_conv(1, z) * short_conv(2, z)).astype(BF16)

    def make_gate(z):
        return (cot_ref[:, lanes(z)].astype(F32) * short_conv(0, z)).astype(BF16)

    def packed(g):
        mine = pl.ds(pl.multiple_of(g * chans, chans), chans)
        return turn[:, mine, :].reshape(zs * chans, tokens).astype(BF16)

    def picked(z):
        parts = [rows[pl.ds(pl.multiple_of((g * zs + z) * chans, chans), chans), :] for g in range(groups)]
        return jnp.concatenate(parts, axis=0)

    def to_plane(unit):
        @pl.loop(1, groups)
        def _(step):
            g = g_peer(step)
            p_out[unit, g] = packed(g)
            p_copy(unit, g).start()

        p_in[unit, my_g] = packed(my_g)

    def from_plane(unit):
        @pl.loop(1, groups)
        def _(step):
            p_arrival(unit, g_peer(groups - step)).wait_recv()

        @pl.loop(0, groups)
        def _(g):
            rows[pl.ds(pl.multiple_of(g * zs * chans, zs * chans), zs * chans), :] = p_in[unit, g].astype(F32)

    def to_line(unit, block, held_back=0):
        @pl.loop(1, zs - held_back)
        def _(step):
            z = z_peer(step)
            z_out[unit, z] = block(z).astype(BF16)
            z_copy(unit, z).start()

        if held_back:
            @pl.loop(zs - held_back, zs)
            def _(step):
                z = z_peer(step)
                z_out[unit, z] = block(z).astype(BF16)

        z_in[unit, my_z] = block(my_z).astype(BF16)

    def send_held_back(unit, held_back):
        @pl.loop(zs - held_back, zs)
        def _(step):
            z_copy(unit, z_peer(step)).start()

    def from_line(unit, use):
        use(my_z, z_in[unit, my_z].astype(F32))

        @pl.loop(1, zs)
        def _(step):
            z = z_peer(zs - step)
            z_arrival(unit, z).wait_recv()
            use(z, z_in[unit, z].astype(F32))

    def keep(z, block):
        turn[z] = block

    def keep_turned(z, block):
        turn[z] = block.T

    def keep_rows(z, block):
        for g in range(groups):
            rows[pl.ds(pl.multiple_of((g * zs + z) * chans, chans), chans), :] = block[g * chans:(g + 1) * chans]

    def picked_turned(z):
        return picked(z).T

    def forward(spec):
        for c in range(chans):
            signal = rows[pl.ds(c, blocks, stride=chans), :].astype(BF16)
            outer = dot(fwd_outer[...], jnp.concatenate([signal, signal], axis=0))
            real, imag = outer[:blocks], outer[blocks:]
            cos, sin = twists[0], twists[1]
            high, low = split(jnp.concatenate([real * cos + imag * sin, imag * cos - real * sin], axis=1))
            spec[c] = dot(high, fwd_inner[0]) + dot(low, fwd_inner[0]) + dot(high, fwd_inner[1])

    def inverse(multiply, left, right, factor):
        for c in range(chans):
            high, low = split(multiply(left[c], right[c]))
            inner = dot(high, inv_inner[0]) + dot(low, inv_inner[0]) + dot(high, inv_inner[1])
            real, imag = inner[:, :tokens], inner[:, tokens:]
            cos, sin = twists[0], twists[1]
            high, low = split(jnp.concatenate([real * cos - imag * sin, imag * cos + real * sin], axis=0))
            signal = dot(inv_outer[0], high) + dot(inv_outer[1], high) + dot(inv_outer[0], low)
            if factor != 1.0:
                signal = signal * factor
            rows[pl.ds(c, blocks, stride=chans), :] = signal

    def times(left, right):
        lr, li, rr, ri = left[:, :tokens], left[:, tokens:], right[:, :tokens], right[:, tokens:]
        return jnp.concatenate([lr * rr - li * ri, lr * ri + li * rr], axis=1)

    def conj_times(left, right):
        lr, li, rr, ri = left[:, :tokens], left[:, tokens:], right[:, :tokens], right[:, tokens:]
        return jnp.concatenate([lr * rr + li * ri, lr * ri - li * rr], axis=1)

    def rows_to_plane(unit):
        def block(g):
            return rows[pl.ds(pl.multiple_of(g * zs * chans, zs * chans), zs * chans), :].astype(BF16)

        @pl.loop(1, groups)
        def _(step):
            g = g_peer(step)
            p_out[unit, g] = block(g)
            p_copy(unit, g).start()

        p_in[unit, my_g] = block(my_g)

    for unit, make in ((PRODUCT, make_product), (GATE, make_gate)):
        @pl.loop(0, zs)
        def _(z):
            keep_turned(z, make(z).astype(F32))

        to_plane(unit)

    for copy in loads[6:]:
        copy.wait()
    from_plane(PRODUCT)
    to_line(PRODUCT, picked)
    from_line(FILTER, keep_turned)
    to_plane(FILTER)
    from_plane(GATE)
    to_line(GATE, picked)
    from_plane(FILTER)
    forward(spec_h)
    from_line(PRODUCT, keep_rows)
    forward(spec_x)
    inverse(times, spec_x, spec_h, 1.0)
    to_line(CONV, picked)
    from_line(GATE, keep_rows)
    forward(spec_g)
    inverse(conj_times, spec_h, spec_g, 1.0)
    rows_to_plane(DCONV)
    inverse(conj_times, spec_x, spec_g, scale)
    rows_to_plane(DFILTER)
    from_plane(DCONV)
    to_line(DCONV, picked_turned)
    from_line(CONV, keep)
    to_plane(CONV)

    def z_wait(unit):
        @pl.loop(1, zs)
        def _(step):
            z_arrival(unit, z_peer(zs - step)).wait_recv()

    def edge_copy(i):
        return send(
            pre.at[i, :, pl.ds(0, 8)], pre.at[i, :, pl.ds(tokens, 8)], pre_send.at[i], pre_recv.at[i], before
        )

    def tap_sums(i, z):
        own = pre[i, z, pl.ds(0, tokens)]
        for tap in range(3):
            summed = jnp.sum(own * ext[i, z, pl.ds(8 - tap, tokens)], axis=0, keepdims=True)
            part[3 * i + tap, pl.ds(z, 1)] = summed * scale

    def reverse_conv(i, out_ref):
        @pl.loop(0, zs)
        def _(z):
            pre[i, z, pl.ds(tokens, 8)] = pre[i, z, pl.ds(tokens, 8)] * precedes
            summed = weights_ref[i, pl.ds(0, 1), lanes(z)] * pre[i, z, pl.ds(0, tokens)]
            for tap in (1, 2):
                summed = summed + weights_ref[i, pl.ds(tap, 1), lanes(z)] * pre[i, z, pl.ds(tap, tokens)]
            out_ref[:, lanes(z)] = summed.astype(BF16)

    from_plane(CONV)

    @pl.loop(0, zs)
    def _(z):
        conv = picked_turned(z)
        gated_ref[:, lanes(z)] = (shorts[0, z] * conv).astype(BF16)
        pre[0, z, pl.ds(0, tokens)] = cot_ref[:, lanes(z)].astype(F32) * conv

    unloads[0].start()
    edge_copy(0).start()
    part[...] = jnp.zeros_like(part)

    @pl.loop(0, zs)
    def _(z):
        tap_sums(0, z)

    edge_copy(0).wait()
    reverse_conv(0, qgrad_ref)
    unloads[1].start()
    from_plane(DFILTER)
    late = 3 * zs // 8
    to_line(DFILTER, picked_turned, late)

    z_wait(DCONV)

    @pl.loop(0, zs)
    def _(z):
        grad = z_in[DCONV, z].astype(F32)
        pre[1, z, pl.ds(0, tokens)] = grad * shorts[2, z]
        pre[2, z, pl.ds(0, tokens)] = grad * shorts[1, z]

    edge_copy(1).start()
    edge_copy(2).start()

    share = part.shape[0] // groups

    def shares(g):
        return pl.ds(g * share, share)

    def part_copy(g, slot):
        return send(part.at[shares(g)], part_in.at[slot], part_send.at[g], part_recv.at[slot], at_g(g))

    def line_copy(z, slot):
        return send(plane, line_in.at[slot], line_send.at[z], line_recv.at[slot], at_z(z))

    def total_copy(g, slot):
        return send(total, total_in.at[shares(slot)], total_send.at[g], total_recv.at[slot], at_g(g))

    @pl.loop(0, zs)
    def _(z):
        tap_sums(1, z)
        tap_sums(2, z)

    active = -(-9 // share)
    part_in[my_g] = part[shares(my_g)]

    @pl.loop(0, active)
    def _(g):
        @pl.when(g != my_g)
        def _():
            part_copy(g, my_g).start()

    @pl.when(my_g < active)
    def _():
        @pl.loop(1, groups)
        def _(step):
            g = g_peer(groups - step)
            part_copy(g, g).wait_recv()

        plane[...] = jnp.sum(part_in[...], axis=0)

        @pl.loop(1, zs)
        def _(step):
            line_copy(z_peer(step), my_z).start()

        line_in[my_z] = plane[...]

    send_held_back(DFILTER, late)
    edge_copy(1).wait()
    reverse_conv(1, kgrad_ref)
    unloads[2].start()
    edge_copy(2).wait()
    reverse_conv(2, vgrad_ref)
    unloads[3].start()

    @pl.when(my_g < active)
    def _():
        @pl.loop(1, zs)
        def _(step):
            z = z_peer(zs - step)
            line_copy(z, z).wait_recv()

        total[...] = jnp.sum(line_in[...], axis=0)

        @pl.loop(1, groups)
        def _(step):
            total_copy(g_peer(step), my_g).start()

        total_in[shares(my_g)] = total[...]

    z_wait(DFILTER)

    @pl.loop(0, zs)
    def _(z):
        fgrad_ref[:, lanes(z)] = z_in[DFILTER, z].astype(F32)

    unloads[4].start()

    @pl.loop(0, active)
    def _(g):
        @pl.when(g != my_g)
        def _():
            total_copy(g, g).wait_recv()

    for z in range(zs):
        for i in range(3):
            for tap in range(3):
                sgrad_ref[i, tap:tap + 1, z * LANES:(z + 1) * LANES] = total_in[3 * i + tap, z:z + 1]

    unloads[5].start()

    @pl.loop(0, active)
    def _(g):
        @pl.when(g != my_g)
        def _():
            part_copy(g, my_g).wait_send()

    @pl.when(my_g < active)
    def _():
        @pl.loop(1, zs)
        def _(step):
            line_copy(z_peer(step), my_z).wait_send()

        @pl.loop(1, groups)
        def _(step):
            total_copy(g_peer(step), my_g).wait_send()

    @pl.loop(0, 6)
    def _(unit):
        @pl.loop(1, zs)
        def _(step):
            z_copy(unit, z_peer(step)).wait_send()

        @pl.loop(1, groups)
        def _(step):
            p_copy(unit, g_peer(step)).wait_send()

    for copy in unloads:
        copy.wait()


def store(*refs):
    *refs, sems = refs
    count = len(refs) // 3
    sources, targets, held = refs[:count], refs[count:2 * count], refs[2 * count:]
    loads = [pltpu.make_async_copy(sources[i], held[i], sems.at[0, i]) for i in range(count)]
    stores = [pltpu.make_async_copy(held[i], targets[i], sems.at[1, i]) for i in range(count)]
    for copy in loads:
        copy.start()
    for load, copy in zip(loads, stores):
        load.wait()
        copy.start()
    for copy in stores:
        copy.wait()


def shards(factors, query_proj, key_proj, value_proj, cotangent, filter_taps, short_weights):
    ys, zs, xs = factors
    blocks = ys * zs * xs
    groups = ys * xs
    tokens, width = query_proj.shape
    chans = LANES // groups
    scale = 1.0 / math.sqrt(blocks * tokens)
    far = pl.BlockSpec(memory_space=pltpu.HBM)
    constants = [jnp.asarray(table) for table in tables(factors)]
    operands = (query_proj, key_proj, value_proj, cotangent, filter_taps, short_weights, *constants)
    token_out = jax.ShapeDtypeStruct((tokens, width), BF16)
    outs = (
        token_out, token_out, token_out, token_out,
        jax.ShapeDtypeStruct((tokens, width), F32),
        jax.ShapeDtypeStruct(short_weights.shape, F32),
    )
    share = -(-9 // groups)
    scratch = [pltpu.VMEM(array.shape, array.dtype) for array in (*operands, *outs)]
    scratch += [
        pltpu.VMEM((3, 16, width), BF16),
        pltpu.VMEM((3, zs, tokens + 8, LANES), F32),
        pltpu.VMEM((3, zs, tokens, LANES), F32),
        pltpu.VMEM((3, zs, tokens + 8, LANES), F32),
        pltpu.VMEM((6, zs, tokens, LANES), BF16),
        pltpu.VMEM((6, zs, tokens, LANES), BF16),
        pltpu.VMEM((6, groups, zs * chans, tokens), BF16),
        pltpu.VMEM((6, groups, zs * chans, tokens), BF16),
        pltpu.VMEM((zs, LANES, tokens), F32),
        pltpu.VMEM((blocks * chans, tokens), F32),
        pltpu.VMEM((chans, blocks, 2 * tokens), F32),
        pltpu.VMEM((chans, blocks, 2 * tokens), F32),
        pltpu.VMEM((chans, blocks, 2 * tokens), F32),
        pltpu.VMEM((groups * share, zs, LANES), F32),
        pltpu.VMEM((groups, share, zs, LANES), F32),
        pltpu.VMEM((share, zs, LANES), F32),
        pltpu.VMEM((zs, share, zs, LANES), F32),
        pltpu.VMEM((share, zs, LANES), F32),
        pltpu.VMEM((groups * share, zs, LANES), F32),
    ]
    for shape in (
        (len(operands),), (len(outs),), (3,), (3,), (3,), (3,), (6, zs), (6, zs), (6, groups), (6, groups),
        (groups,), (groups,), (zs,), (zs,), (groups,), (groups,),
    ):
        scratch.append(pltpu.SemaphoreType.DMA(shape))
    results = pl.pallas_call(
        functools.partial(kernel, factors, scale),
        out_shape=outs,
        in_specs=[far] * len(operands),
        out_specs=(far,) * len(outs),
        scratch_shapes=scratch,
        compiler_params=pltpu.CompilerParams(
            collective_id=0, has_side_effects=True, vmem_limit_bytes=VMEM_BYTES
        ),
    )(*operands)
    return pl.pallas_call(
        store,
        out_shape=outs,
        in_specs=[far] * len(outs),
        out_specs=(far,) * len(outs),
        scratch_shapes=[pltpu.VMEM(out.shape, out.dtype) for out in outs] + [pltpu.SemaphoreType.DMA((2, len(outs)))],
    )(*results)


def solution(mesh):
    rows = P("ctx", "tp")
    weights = P(None, None, "tp")
    return jax.shard_map(
        functools.partial(shards, FACTORS[mesh.shape["ctx"]]),
        mesh=mesh,
        in_specs=(rows, rows, rows, rows, rows, weights),
        out_specs=(rows, rows, rows, rows, rows, weights),
        check_vma=False,
    )
```
